32 devices in a mesh: section: 4 (over x, core), cls: 8 (over z, y).
Axes of the slice: x: 2, y: 2, z: 4, core: 2. Of those that a mesh axis runs over, the one named last changes fastest.
Arguments:
- images: bfloat16 [512, 256, 256], P(('section', 'cls')), may hold values from -6 to 6
- group_ids: int32 [512], P(('section', 'cls')), may hold values from 0 to 3
- row_filters: bfloat16 [4, 256, 256], replicated, may hold values from -0.375 to 0.375
- column_filters: bfloat16 [4, 256, 256], replicated, may hold values from -0.375 to 0.375
- basis_rows: bfloat16 [256, 16], replicated, may hold values from -0.375 to 0.375
- basis_columns: bfloat16 [256, 16], replicated, may hold values from -0.375 to 0.375
- rotations: bfloat16 [36, 256, 256], P('section'), may hold values from -0.375 to 0.375
- references: bfloat16 [16, 256], P('cls'), may hold values from -2 to 2
- sharpness: bfloat16 [512], P(('section', 'cls')), may hold values from 0.049804688 to 2
- best_rotation: int32 [512], P(('section', 'cls')), may hold values from 0 to 35
- assignments: int32 [512, 16], P(('section', 'cls')), may hold values from 0 to 15, all different within a row; in each aligned block of 16 rows (0 to 15, 16 to 31, ...) at most 16 rows name the same one
Outputs:
- new_references: float32 [16, 256], P('cls')
- evidence: float32 [512], P(('section', 'cls'))
The draws below stay inside these ranges and needn't reach their ends.
Inputs may be any that keep to these rules, and one draw needn't show every extreme that they name: `assignments`: each particle lists 16 different classes; among the particles of one device no class is listed more than 16 times, a bound that some block reaches.
All inputs are finite; a program needn't handle non-finite values.
Results may differ from the reference program's by a relative error of at most 0.019.
Values may be sent and summed in bfloat16 or wider, within the bound.
No kernel may reach another device: no remote copies, remote signals or barrier semaphores. Data moves between devices by JAX's collectives and lax.ppermute only.
A program may use at most 64 MiB of HBM per device.

```python
import math
import jax
import jax.numpy as jnp
import numpy as np
from jax import lax

PIX = 256
NB = 16
COEF = 256
ROT = 36
GROUPS = 4
PART_DEV = 16
CLASSES = 16
TOP = 16
PARTICLES = 512
MOST = 16


def touch_ends(array, stream_key, low, top_value):
    longest = array.shape.index(max(array.shape))
    spots = []
    for shift in (0, 1):
        where = [jax.random.randint(jax.random.fold_in(stream_key, axis), (), 0, length) for axis, length in enumerate(array.shape)]
        where[longest] = (where[longest] + shift) % array.shape[longest]
        spots.append(tuple(where))
    return array.at[spots[0]].set(low).at[spots[1]].set(top_value)


def block_levels(own_key, dims, pieces, low, largest):
    loudness, own = 1.0, jax.random.fold_in(own_key, 6)
    for axis_at, parts in pieces:
        draws = jnp.exp(jax.random.uniform(jax.random.fold_in(own, axis_at), (parts,), jnp.float32, low / len(pieces), largest / len(pieces)))
        loudness = loudness * jnp.repeat(draws, dims[axis_at] // parts).reshape([-1 if axis == axis_at else 1 for axis in range(len(dims))])
    return loudness


def assign_block(stream_key, own, number, rows, number_of, top, bound, lean):
    sequence = jax.random.permutation(stream_key, number_of)
    crowded, ordinary = portions_of(number_of, rows * top, bound, lean, True), portions_of(number_of, rows * top, bound, lean, False)
    places = jnp.arange(number_of)

    def named(lengths, turn):
        used = int((lengths > 0).sum())
        fixed = max(1, used // 4)
        moved = fixed + (places - fixed + turn * (used - fixed)) % max(1, number_of - fixed)
        return jnp.zeros((number_of,), jnp.int32).at[sequence[jnp.where(places < fixed, places, moved)]].set(jnp.asarray(lengths, jnp.int32))

    lengths = jnp.where(number % 4 == 0, named(crowded, number // 4), named(ordinary, number - number // 4 - 1))
    mixed = jax.random.permutation(jax.random.fold_in(own, 3), number_of)
    source_of, sink = mixed[0:number_of // 2 * 2:2], mixed[1:number_of // 2 * 2:2]
    margin = jnp.minimum(lengths[source_of] - 1, bound - lengths[sink]) // 2
    margin = jnp.where((source_of == sequence[0]) | (sink == sequence[0]) | (lengths[sink] == 0), 0, jnp.maximum(margin, 0))
    moved = jax.random.randint(jax.random.fold_in(own, 4), (number_of // 2,), 0, 1 << 20) % (margin + 1)
    lengths = lengths.at[source_of].add(-moved).at[sink].add(moved)
    items = jnp.searchsorted(jnp.cumsum(lengths), jnp.arange(rows * top), side="right").astype(jnp.int32)
    grid = items.reshape(top, rows).T
    grid = grid[jax.random.permutation(jax.random.fold_in(own, 1), rows)]
    turn = jax.random.randint(jax.random.fold_in(own, 2), (rows, 1), 0, top)
    return jnp.take_along_axis(grid, (jnp.arange(top)[None, :] + turn) % top, axis=1)


def portions_of(amount, total, bound, slope, full):
    loads = [(1 << 20) // math.isqrt(rank ** slope) + 1 for rank in range(1, amount + 1)]
    largest = bound if full else min(bound, max(-(-total // amount), total * loads[0] // sum(loads)))
    least = 1 if total - largest >= amount - 1 else 0
    holding, surplus = [largest] + [least] * (amount - 1), total - largest - least * (amount - 1)
    while surplus > 0:
        candidates = [i for i in range(1, amount) if holding[i] < largest] or [i for i in range(1, amount) if holding[i] < bound]
        whole, left = sum([loads[i] for i in candidates]), surplus
        for i in candidates:
            extra = min(bound - holding[i], max(1, left * loads[i] // whole), surplus)
            holding[i] = holding[i] + extra
            surplus = surplus - extra
    return np.array(holding)


def noise(key, dims, scale, most, split=(), kind=jnp.bfloat16):
    array = scale * jax.random.normal(key, dims, jnp.float32)
    if split:
        array = array * block_levels(key, dims, split, -0.22, 0.18)
    return jnp.clip(array, -most, most).astype(kind)


def setup_inputs(seed: int = 0) -> dict:
    streams_of = jax.random.split(jax.random.key(seed), 12)
    images = noise(streams_of[0], (PARTICLES, PIX, PIX), 1.0, 6.0, ((0, 32),))
    group_ids = touch_ends(jax.random.randint(streams_of[1], (PARTICLES,), 0, GROUPS), jax.random.fold_in(streams_of[1], 1), 0, GROUPS - 1).astype(jnp.int32)
    row_filters = noise(streams_of[2], (GROUPS, PIX, PIX), PIX ** -0.5, 0.375)
    column_filters = noise(streams_of[3], (GROUPS, PIX, PIX), PIX ** -0.5, 0.375)
    basis_rows = noise(streams_of[4], (PIX, NB), PIX ** -0.5, 0.375)
    basis_columns = noise(streams_of[5], (PIX, NB), PIX ** -0.5, 0.375)
    rotations = noise(streams_of[6], (ROT, COEF, COEF), COEF ** -0.5, 0.375, ((0, 4),))
    references = noise(streams_of[7], (CLASSES, COEF), 0.125, 2.0, ((0, 8),))
    sharpness = jnp.clip(jnp.exp(math.log(2.0) - 3.6927934 * jax.random.uniform(streams_of[8], (PARTICLES,), jnp.float32) ** block_levels(streams_of[8], (PARTICLES,), ((0, 32),), -0.2, 0.2)), 0.049804688, 2.0).astype(jnp.bfloat16)
    best_rotation = touch_ends(jax.random.randint(streams_of[9], (PARTICLES,), 0, ROT), jax.random.fold_in(streams_of[9], 1), 0, ROT - 1).astype(jnp.int32)
    assignments_keys = jax.random.split(jax.random.fold_in(streams_of[10], 1), PARTICLES // PART_DEV)
    assignments_turns = jax.random.permutation(jax.random.fold_in(streams_of[10], 3), PARTICLES // PART_DEV)
    assignments = jax.vmap(lambda own, number: assign_block(jax.random.fold_in(streams_of[10], 2), own, number, PART_DEV, CLASSES, TOP, MOST, 2))(assignments_keys, assignments_turns).reshape((PARTICLES, TOP))
    return {"images": images, "group_ids": group_ids, "row_filters": row_filters, "column_filters": column_filters, "basis_rows": basis_rows, "basis_columns": basis_columns, "rotations": rotations, "references": references, "sharpness": sharpness, "best_rotation": best_rotation, "assignments": assignments}


EPSILON = 1e-05

def soft_edge(pixels):
    coordinate = (jnp.arange(pixels, dtype=jnp.float32) - (pixels - 1) / 2.0) / (pixels / 2.0)
    radius = jnp.sqrt(coordinate[:, None] * coordinate[:, None] + coordinate[None, :] * coordinate[None, :])
    falloff = jnp.clip((radius - 0.8) / 0.15, 0.0, 1.0)
    return 0.5 + 0.5 * jnp.cos(math.pi * falloff)

def filter_reference(block_images, block_groups, row_filters, column_filters, basis_rows, basis_columns):
    column_each = jnp.take(column_filters, block_groups, axis=0).astype(jnp.float32)
    row_each = jnp.take(row_filters, block_groups, axis=0).astype(jnp.float32)
    filtered_half = jnp.einsum('bij,bjk->bik', block_images.astype(jnp.float32), column_each).astype(jnp.bfloat16)
    filtered = jnp.einsum('bij,bjk->bik', row_each, filtered_half.astype(jnp.float32))
    masked = filtered * soft_edge(block_images.shape[1])
    power = lax.optimization_barrier(jnp.mean(masked * masked, axis=(1, 2), keepdims=True))
    normed = (masked * lax.rsqrt(power + EPSILON)).astype(jnp.bfloat16)
    inner = jnp.einsum('bij,jk->bik', normed.astype(jnp.float32), basis_columns.astype(jnp.float32))
    coeffs = jnp.einsum('ja,bjk->bak', basis_rows.astype(jnp.float32), inner, precision=lax.Precision.HIGHEST)
    return coeffs.reshape(coeffs.shape[0], -1).astype(jnp.bfloat16)

def reference(images, group_ids, row_filters, column_filters, basis_rows, basis_columns, rotations, references, sharpness, best_rotation, assignments):
    blocks = PARTICLES // PART_DEV

    def one_block(block_inputs):
        block_images, block_groups, block_sharpness, block_best, block_assign = block_inputs
        coeffs = filter_reference(block_images, block_groups, row_filters, column_filters, basis_rows, basis_columns)
        turned = jnp.einsum('rkl,nl->nrk', rotations.astype(jnp.float32), coeffs.astype(jnp.float32)).astype(jnp.bfloat16)
        scores = jnp.einsum('nrk,ck->nrc', turned.astype(jnp.float32), references.astype(jnp.float32))
        scores = scores * block_sharpness.astype(jnp.float32)[:, None, None]
        log_marg = jax.nn.logsumexp(scores, axis=1)
        evidence = jax.nn.logsumexp(log_marg, axis=1)
        matches = block_assign[:, :, None] == jnp.arange(CLASSES, dtype=jnp.int32)[None, None, :]
        picked = lax.optimization_barrier(jnp.sum(jnp.where(matches, log_marg[:, None, :], 0.0), axis=2))
        weights = jax.nn.softmax(picked, axis=1).astype(jnp.bfloat16)
        aligned = jnp.take_along_axis(turned, block_best.astype(jnp.int32)[:, None, None], axis=1)[:, 0, :]
        contribution = (weights.astype(jnp.float32)[:, :, None] * aligned.astype(jnp.float32)[:, None, :]).astype(jnp.bfloat16)
        return (evidence, contribution, weights)
    block_inputs = (images.reshape(blocks, PART_DEV, PIX, PIX), group_ids.reshape(blocks, PART_DEV), sharpness.reshape(blocks, PART_DEV), best_rotation.reshape(blocks, PART_DEV), assignments.reshape(blocks, PART_DEV, TOP))
    evidence, contribution, weights = lax.map(one_block, block_inputs)
    flat_classes = assignments.reshape(-1)
    class_sums = jax.ops.segment_sum(contribution.reshape(-1, COEF).astype(jnp.float32), flat_classes, num_segments=CLASSES)
    class_weights = jax.ops.segment_sum(weights.reshape(-1).astype(jnp.float32), flat_classes, num_segments=CLASSES)
    new_references = (class_sums + references.astype(jnp.float32)) / (class_weights[:, None] + 1.0)
    return (new_references, evidence.reshape(-1))
```

```python
import math

import jax
import jax.numpy as jnp
import numpy as np
from jax import lax
from jax.experimental import pallas as pl
from jax.experimental.pallas import tpu as pltpu
from jax.sharding import PartitionSpec as P

EPSILON = 1e-05
LANES = 128
BF16 = jnp.bfloat16
F32 = jnp.float32


def soft_edge(pixels):
    coordinate = (np.arange(pixels, dtype=np.float32) - (pixels - 1) / 2.0) / (pixels / 2.0)
    radius = np.sqrt(coordinate[:, None] ** 2 + coordinate[None, :] ** 2)
    falloff = np.clip((radius - 0.8) / 0.15, 0.0, 1.0)
    return (0.5 + 0.5 * np.cos(math.pi * falloff)).astype(np.float32)


def filter_kernel(
    batch,
    own_classes,
    classes,
    groups_ref,
    best_ref,
    images_ref,
    row_ref,
    column_ref,
    mask_ref,
    basis_rows_ref,
    basis_columns_ref,
    assignments_ref,
    sharp_ref,
    out_ref,
    inner,
):
    step = pl.program_id(0)
    pixels = mask_ref.shape[0]
    row_count = basis_rows_ref.shape[0]
    column_count = basis_columns_ref.shape[0]
    width = row_count * column_count
    particles, message = out_ref.shape

    group = [groups_ref[step * batch + b] for b in range(batch)]
    half = [
        jnp.dot(images_ref[b], column_ref[group[b]], preferred_element_type=F32).astype(BF16)
        for b in range(batch)
    ]
    scale = []
    masked = []
    for b in range(batch):
        filtered = jnp.dot(row_ref[group[b]], half[b], preferred_element_type=F32) * mask_ref[...]
        power = jnp.sum(filtered * filtered, axis=0, keepdims=True)
        power = jnp.sum(power, axis=1, keepdims=True) * (1.0 / (pixels * pixels))
        scale.append(lax.rsqrt(power + EPSILON))
        masked.append(filtered.astype(BF16))
    for b in range(batch):
        rows = jnp.dot(basis_rows_ref[...], masked[b], preferred_element_type=F32)
        place = pl.multiple_of((step * batch + b) * row_count, row_count)
        inner[pl.ds(place, row_count), :] = rows * scale[b]

    @pl.when(step == pl.num_programs(0) - 1)
    def _():
        lane = lax.broadcasted_iota(jnp.int32, (column_count, width), 1)
        which = lax.broadcasted_iota(jnp.int32, (column_count, width), 0)
        spread = (lane % column_count == which).astype(F32).astype(BF16)
        wide = lax.dot_general(
            basis_columns_ref[...], spread, (((0,), (0,)), ((), ())), preferred_element_type=F32
        ).astype(BF16)
        held = inner[...]
        high = held.astype(BF16)
        low = (held - high.astype(F32)).astype(BF16)
        both = jnp.dot(high, wide, preferred_element_type=F32)
        both = both + jnp.dot(low, wide, preferred_element_type=F32)
        lane = lax.broadcasted_iota(jnp.int32, both.shape, 1)
        which = lax.broadcasted_iota(jnp.int32, both.shape, 0)
        both = jnp.where(lane // column_count == which % row_count, both, 0.0)
        coeffs = jnp.sum(both.reshape(particles, row_count, width), axis=1)

        lane = lax.broadcasted_iota(jnp.int32, (particles, message - width), 1)
        place = lax.broadcasted_iota(jnp.int32, (particles, message - width), 0)
        named = (lane // own_classes ^ lax.axis_index("cls")) * own_classes + lane % own_classes
        named = jnp.where(lane < classes, named, -1)
        meta = jnp.zeros(lane.shape, F32)
        assignments = assignments_ref[...]
        for j in range(assignments.shape[1]):
            meta = jnp.where(assignments[:, j : j + 1] == named, 1.0, meta)
        square = (particles, particles)
        same = lax.broadcasted_iota(jnp.int32, square, 0) == lax.broadcasted_iota(
            jnp.int32, square, 1
        )
        sharp = jnp.broadcast_to(sharp_ref[...].astype(F32), square)
        sharp = jnp.sum(jnp.where(same, sharp, 0.0), axis=1, keepdims=True)
        meta = jnp.where(lane == classes, sharp, meta)
        for n in range(particles):
            meta = jnp.where(
                (place == n) & (lane == classes + 1), best_ref[n].astype(F32), meta
            )
        out_ref[...] = jnp.concatenate([coeffs.astype(BF16), meta.astype(BF16)], axis=1)


def filter_images(
    images,
    group_ids,
    row_filters,
    column_filters,
    basis_rows,
    basis_columns,
    sharpness,
    best_rotation,
    assignments,
    own_classes,
    classes,
):
    particles, pixels = images.shape[:2]
    groups = row_filters.shape[0]
    row_count, column_count = basis_rows.shape[1], basis_columns.shape[1]
    message = row_count * column_count + classes + 2
    message += -message % LANES
    batch = 8 if particles % 8 == 0 else 1
    mask = jnp.asarray(soft_edge(pixels))
    whole2 = lambda s, *_: (0, 0)
    whole3 = lambda s, *_: (0, 0, 0)
    return pl.pallas_call(
        lambda *refs: filter_kernel(batch, own_classes, classes, *refs),
        out_shape=pltpu.VMEM((particles, message), BF16),
        grid_spec=pltpu.PrefetchScalarGridSpec(
            num_scalar_prefetch=2,
            grid=(particles // batch,),
            in_specs=[
                pl.BlockSpec((batch, pixels, pixels), lambda s, *_: (s, 0, 0)),
                pl.BlockSpec((groups, pixels, pixels), whole3),
                pl.BlockSpec((groups, pixels, pixels), whole3),
                pl.BlockSpec((pixels, pixels), whole2),
                pl.BlockSpec((row_count, pixels), whole2),
                pl.BlockSpec((column_count, pixels), whole2),
                pl.BlockSpec(assignments.shape, whole2),
                pl.BlockSpec((1, particles), whole2),
            ],
            out_specs=pl.BlockSpec((particles, message), whole2),
            scratch_shapes=[pltpu.VMEM((particles * row_count, pixels), F32)],
        ),
        compiler_params=pltpu.CompilerParams(
            dimension_semantics=("arbitrary",), vmem_limit_bytes=60 * 1024 * 1024
        ),
        cost_estimate=pl.CostEstimate(
            flops=4 * particles * pixels**3,
            bytes_accessed=2 * pixels * pixels * (particles + 2 * groups),
            transcendentals=0,
        ),
        name="filter_images",
    )(
        group_ids,
        best_rotation,
        images,
        row_filters,
        column_filters,
        mask,
        basis_rows.T,
        basis_columns.T,
        assignments,
        sharpness.reshape(1, particles),
    )


def cross(array, distance):
    sections, owners = lax.axis_size("section"), lax.axis_size("cls")
    pairs = [
        (s * owners + c, (s ^ 1) * owners + (c ^ distance))
        for s in range(sections)
        for c in range(owners)
    ]
    return lax.ppermute(array, ("section", "cls"), pairs)


def swap(array, axis, distance):
    size = lax.axis_size(axis)
    return lax.ppermute(array, axis, [(i, i ^ distance) for i in range(size)])


def log_add(a, b):
    top = jnp.maximum(a, b)
    return top + jnp.log(jnp.exp(a - top) + jnp.exp(b - top))


def iotas(shape):
    return lax.broadcasted_iota(jnp.int32, shape, 0), lax.broadcasted_iota(jnp.int32, shape, 1)


def one_hot(condition):
    return condition.astype(F32).astype(BF16)


def over_lanes(a, b):
    return lax.dot_general(a, b, (((1,), (1,)), ((), ())), preferred_element_type=F32)


def split_lanes(values, lanes):
    count = values.shape[1]
    high = values.astype(BF16)
    rest = values - high.astype(F32)
    middle = rest.astype(BF16)
    low = (rest - middle.astype(F32)).astype(BF16)
    k, lane = iotas((count, lanes))
    spread = jnp.dot(high, one_hot(lane == k), preferred_element_type=F32)
    spread = spread + jnp.dot(middle, one_hot(lane == k + count), preferred_element_type=F32)
    spread = spread + jnp.dot(low, one_hot(lane == k + 2 * count), preferred_element_type=F32)
    return spread.astype(BF16)


def join_lanes(parts, count, block, distance):
    k, n = iotas((parts.shape[1], count))
    source = (n // block ^ distance) * block + n % block
    here = (k == source) | (k == source + count) | (k == source + 2 * count)
    return jnp.dot(parts, one_hot(here), preferred_element_type=F32)


def score_kernel(
    particles, sections, classes, mine_ref, theirs_ref, own_ref, sibling_ref, out_ref, listed_ref
):
    local_rotations, width, _ = own_ref.shape
    section = lax.axis_index("section")
    held = sections * particles
    half = sections // 2
    rows = mine_ref.shape[0] // half
    spare = rows - particles
    fetched = classes // sections

    coeffs, meta, stack = [], [], []
    for m in range(sections):
        source = mine_ref if m < half else theirs_ref
        base = (m if m < half else sections - 1 - m) * rows
        coeffs.append(source[base : base + particles, :width])
        meta.append(source[base : base + particles, width:])
        stack.append(source[base + particles : base + rows, :width])
    coeffs = jnp.concatenate(coeffs, axis=0)
    meta = jnp.concatenate(meta, axis=0)
    stack = jnp.concatenate(stack, axis=0)

    q, k = iotas((classes, sections * spare))
    place = (k // spare ^ section) * fetched + k % spare
    refs = jnp.dot(
        one_hot((q == place) & (k % spare < fetched)), stack, preferred_element_type=F32
    ).astype(BF16)

    q, k = iotas((classes + 16, meta.shape[1]))
    turned_meta = over_lanes(one_hot(q == k), meta)
    listed_ref[...] = turned_meta[:classes]
    sharp = turned_meta[classes : classes + 1]
    best = meta[:, classes + 1 : classes + 2].astype(F32)

    turned_refs = jnp.concatenate(
        [
            jnp.dot(refs, rotations_ref[r], preferred_element_type=F32).astype(BF16)
            for rotations_ref in (own_ref, sibling_ref)
            for r in range(local_rotations)
        ],
        axis=0,
    )
    scores = over_lanes(turned_refs, coeffs) * sharp
    scores = scores.reshape(2 * local_rotations, classes, held)
    top = jnp.max(scores, axis=0)
    marg = top + jnp.log(jnp.sum(jnp.exp(scores - top[None]), axis=0))
    out_ref[held:, :] = split_lanes(marg, width)

    wide = coeffs.astype(F32)
    aligned = jnp.zeros((held, width), F32)
    for owner, rotations_ref in ((section, own_ref), (section ^ 1, sibling_ref)):
        offset = best - (owner * local_rotations).astype(F32)
        for r in range(local_rotations):
            chosen = jnp.where(offset == r, wide, 0.0).astype(BF16)
            aligned = aligned + over_lanes(chosen, rotations_ref[r])
    out_ref[:held, :] = aligned.astype(BF16)


def merge(particles, distance, held, mine_ref, theirs_ref):
    slots = held // particles
    theirs = [
        theirs_ref[(m ^ distance) * particles : (m ^ distance) * particles + particles, :]
        for m in range(slots)
    ]
    aligned = mine_ref[:held, :].astype(F32) + jnp.concatenate(theirs, axis=0).astype(F32)
    marg = log_add(
        join_lanes(mine_ref[held:, :], held, particles, 0),
        join_lanes(theirs_ref[held:, :], held, particles, distance),
    )
    return aligned.astype(BF16), marg


def sums_kernel(particles, distance, held, mine_ref, theirs_ref, listed_ref, out_ref, evidence_ref):
    aligned, marg = merge(particles, distance, held, mine_ref, theirs_ref)
    width = aligned.shape[1]
    top = jnp.max(marg, axis=0, keepdims=True)
    raised = jnp.exp(marg - top)
    evidence_ref[...] = top + jnp.log(jnp.sum(raised, axis=0, keepdims=True))
    picked = jnp.where(listed_ref[...] > 0.0, marg, -jnp.inf)
    raised = jnp.exp(picked - jnp.max(picked, axis=0, keepdims=True))
    weights = raised / jnp.sum(raised, axis=0, keepdims=True)
    weights = weights.astype(BF16)
    out_ref[:, :width] = jnp.dot(weights, aligned, preferred_element_type=F32)
    class_weights = jnp.sum(weights.astype(F32), axis=1, keepdims=True)
    out_ref[:, width:] = jnp.broadcast_to(class_weights, (marg.shape[0], LANES))


def small_call(kernel, name, *operands, out_shape, flops=0):
    read = sum(x.size * x.dtype.itemsize for x in operands)
    return pl.pallas_call(
        kernel,
        out_shape=out_shape,
        in_specs=[pl.BlockSpec(memory_space=pltpu.VMEM)] * len(operands),
        out_specs=jax.tree.map(lambda _: pl.BlockSpec(memory_space=pltpu.VMEM), out_shape),
        compiler_params=pltpu.CompilerParams(vmem_limit_bytes=16 * 1024 * 1024),
        cost_estimate=pl.CostEstimate(flops=flops, bytes_accessed=read, transcendentals=0),
        name=name,
    )(*operands)


def body(
    images,
    group_ids,
    row_filters,
    column_filters,
    basis_rows,
    basis_columns,
    rotations,
    references,
    sharpness,
    best_rotation,
    assignments,
):
    particles = images.shape[0]
    sections = lax.axis_size("section")
    owners = lax.axis_size("cls")
    own_classes, width = references.shape
    classes = own_classes * owners
    held = sections * particles

    sibling_rotations = swap(rotations, "section", 1)

    part = owners // sections
    refs = []
    for j in range(min(part, 2)):
        pairs = [
            (s * owners + c, s * owners + (c ^ (s * part + j or 1)))
            for s in range(sections)
            for c in range(owners)
        ]
        block = lax.ppermute(references, ("section", "cls"), pairs)
        if j == 0:
            block = jnp.where(lax.axis_index("section") == 0, references, block)
        refs.append(block)
    refs = jnp.concatenate(refs, axis=0)
    distance = 2
    while distance < part:
        refs = jnp.concatenate([refs, swap(refs, "cls", distance)], axis=0)
        distance *= 2

    message = filter_images(
        images,
        group_ids,
        row_filters,
        column_filters,
        basis_rows,
        basis_columns,
        sharpness,
        best_rotation,
        assignments,
        own_classes,
        classes,
    )
    refs = jnp.pad(refs, ((0, -refs.shape[0] % 16), (0, message.shape[1] - width)))
    message = jnp.concatenate([message, refs], axis=0)
    message = jnp.concatenate([message, swap(message, "section", 1)], axis=0)
    marg, listed = small_call(
        lambda *r: score_kernel(particles, sections, classes, *r),
        "scores",
        message,
        swap(message, "section", sections - 1),
        rotations,
        sibling_rotations,
        out_shape=(
            jax.ShapeDtypeStruct((held + classes, width), BF16),
            jax.ShapeDtypeStruct((classes, held), F32),
        ),
    )

    sums, evidence = small_call(
        lambda *r: sums_kernel(particles, sections - 1, held, *r),
        "class_sums",
        marg,
        swap(marg, "section", sections - 1),
        listed,
        out_shape=(
            jax.ShapeDtypeStruct((classes, width + LANES), F32),
            jax.ShapeDtypeStruct((1, held), F32),
        ),
    )

    distance = owners // 2
    while distance:
        half = distance * own_classes
        sums = sums[:half] + cross(sums[half:], distance)
        distance //= 2
    new_references = (sums[:, :width] + references.astype(F32)) / (sums[:, width : width + 1] + 1.0)
    return new_references, evidence[0, :particles]


def solution(mesh):
    in_specs = (
        P(("section", "cls"), None, None),
        P(("section", "cls")),
        P(),
        P(),
        P(),
        P(),
        P("section", None, None),
        P("cls", None),
        P(("section", "cls")),
        P(("section", "cls")),
        P(("section", "cls"), None),
    )
    out_specs = (P("cls", None), P(("section", "cls")))
    return jax.shard_map(body, mesh=mesh, in_specs=in_specs, out_specs=out_specs, check_vma=False)
```

```python
import math

import jax
import jax.numpy as jnp
import numpy as np
from jax import lax
from jax.experimental import pallas as pl
from jax.experimental.pallas import tpu as pltpu
from jax.sharding import PartitionSpec as P

EPSILON = 1e-05
LANES = 128
BF16 = jnp.bfloat16
F32 = jnp.float32


def soft_edge(pixels):
    coordinate = (np.arange(pixels, dtype=np.float32) - (pixels - 1) / 2.0) / (pixels / 2.0)
    radius = np.sqrt(coordinate[:, None] ** 2 + coordinate[None, :] ** 2)
    falloff = np.clip((radius - 0.8) / 0.15, 0.0, 1.0)
    return (0.5 + 0.5 * np.cos(math.pi * falloff)).astype(np.float32)


def filter_kernel(
    batch,
    own_classes,
    classes,
    groups_ref,
    best_ref,
    images_ref,
    row_ref,
    column_ref,
    mask_ref,
    basis_rows_ref,
    basis_columns_ref,
    assignments_ref,
    sharp_ref,
    out_ref,
    inner,
):
    step = pl.program_id(0)
    pixels = mask_ref.shape[0]
    row_count = basis_rows_ref.shape[0]
    column_count = basis_columns_ref.shape[0]
    width = row_count * column_count
    particles, message = out_ref.shape

    group = [groups_ref[step * batch + b] for b in range(batch)]
    half = [
        jnp.dot(images_ref[b], column_ref[group[b]], preferred_element_type=F32).astype(BF16)
        for b in range(batch)
    ]
    scale = []
    masked = []
    for b in range(batch):
        filtered = jnp.dot(row_ref[group[b]], half[b], preferred_element_type=F32) * mask_ref[...]
        power = jnp.sum(filtered * filtered, axis=0, keepdims=True)
        power = jnp.sum(power, axis=1, keepdims=True) * (1.0 / (pixels * pixels))
        scale.append(lax.rsqrt(power + EPSILON))
        masked.append(filtered.astype(BF16))
    for b in range(batch):
        rows = jnp.dot(basis_rows_ref[...], masked[b], preferred_element_type=F32)
        place = pl.multiple_of((step * batch + b) * row_count, row_count)
        inner[pl.ds(place, row_count), :] = rows * scale[b]

    @pl.when(step == pl.num_programs(0) - 1)
    def _():
        lane = lax.broadcasted_iota(jnp.int32, (column_count, width), 1)
        which = lax.broadcasted_iota(jnp.int32, (column_count, width), 0)
        spread = (lane % column_count == which).astype(F32).astype(BF16)
        wide = lax.dot_general(
            basis_columns_ref[...], spread, (((0,), (0,)), ((), ())), preferred_element_type=F32
        ).astype(BF16)
        held = inner[...]
        high = held.astype(BF16)
        low = (held - high.astype(F32)).astype(BF16)
        both = jnp.dot(high, wide, preferred_element_type=F32)
        both = both + jnp.dot(low, wide, preferred_element_type=F32)
        lane = lax.broadcasted_iota(jnp.int32, both.shape, 1)
        which = lax.broadcasted_iota(jnp.int32, both.shape, 0)
        both = jnp.where(lane // column_count == which % row_count, both, 0.0)
        coeffs = jnp.sum(both.reshape(particles, row_count, width), axis=1)

        lane = lax.broadcasted_iota(jnp.int32, (particles, message - width), 1)
        place = lax.broadcasted_iota(jnp.int32, (particles, message - width), 0)
        named = (lane // own_classes ^ lax.axis_index("cls")) * own_classes + lane % own_classes
        named = jnp.where(lane < classes, named, -1)
        meta = jnp.zeros(lane.shape, F32)
        assignments = assignments_ref[...]
        for j in range(assignments.shape[1]):
            meta = jnp.where(assignments[:, j : j + 1] == named, 1.0, meta)
        square = (particles, particles)
        same = lax.broadcasted_iota(jnp.int32, square, 0) == lax.broadcasted_iota(
            jnp.int32, square, 1
        )
        sharp = jnp.broadcast_to(sharp_ref[...].astype(F32), square)
        sharp = jnp.sum(jnp.where(same, sharp, 0.0), axis=1, keepdims=True)
        meta = jnp.where(lane == classes, sharp, meta)
        for n in range(particles):
            meta = jnp.where(
                (place == n) & (lane == classes + 1), best_ref[n].astype(F32), meta
            )
        out_ref[...] = jnp.concatenate([coeffs.astype(BF16), meta.astype(BF16)], axis=1)


def filter_images(
    images,
    group_ids,
    row_filters,
    column_filters,
    basis_rows,
    basis_columns,
    sharpness,
    best_rotation,
    assignments,
    own_classes,
    classes,
):
    particles, pixels = images.shape[:2]
    groups = row_filters.shape[0]
    row_count, column_count = basis_rows.shape[1], basis_columns.shape[1]
    message = row_count * column_count + classes + 2
    message += -message % LANES
    batch = 8 if particles % 8 == 0 else 1
    mask = jnp.asarray(soft_edge(pixels))
    whole2 = lambda s, *_: (0, 0)
    whole3 = lambda s, *_: (0, 0, 0)
    return pl.pallas_call(
        lambda *refs: filter_kernel(batch, own_classes, classes, *refs),
        out_shape=pltpu.VMEM((particles, message), BF16),
        grid_spec=pltpu.PrefetchScalarGridSpec(
            num_scalar_prefetch=2,
            grid=(particles // batch,),
            in_specs=[
                pl.BlockSpec((batch, pixels, pixels), lambda s, *_: (s, 0, 0)),
                pl.BlockSpec((groups, pixels, pixels), whole3),
                pl.BlockSpec((groups, pixels, pixels), whole3),
                pl.BlockSpec((pixels, pixels), whole2),
                pl.BlockSpec((row_count, pixels), whole2),
                pl.BlockSpec((column_count, pixels), whole2),
                pl.BlockSpec(assignments.shape, whole2),
                pl.BlockSpec((1, particles), whole2),
            ],
            out_specs=pl.BlockSpec((particles, message), whole2),
            scratch_shapes=[pltpu.VMEM((particles * row_count, pixels), F32)],
        ),
        compiler_params=pltpu.CompilerParams(
            dimension_semantics=("arbitrary",), vmem_limit_bytes=60 * 1024 * 1024
        ),
        cost_estimate=pl.CostEstimate(
            flops=4 * particles * pixels**3,
            bytes_accessed=2 * pixels * pixels * (particles + 2 * groups),
            transcendentals=0,
        ),
        name="filter_images",
    )(
        group_ids,
        best_rotation,
        images,
        row_filters,
        column_filters,
        mask,
        basis_rows.T,
        basis_columns.T,
        assignments,
        sharpness.reshape(1, particles),
    )


def cross(array, distance):
    sections, owners = lax.axis_size("section"), lax.axis_size("cls")
    pairs = [
        (s * owners + c, (s ^ 1) * owners + (c ^ distance))
        for s in range(sections)
        for c in range(owners)
    ]
    return lax.ppermute(array, ("section", "cls"), pairs)


def swap(array, axis, distance):
    size = lax.axis_size(axis)
    return lax.ppermute(array, axis, [(i, i ^ distance) for i in range(size)])


def log_add(a, b):
    top = jnp.maximum(a, b)
    return top + jnp.log(jnp.exp(a - top) + jnp.exp(b - top))


def iotas(shape):
    return lax.broadcasted_iota(jnp.int32, shape, 0), lax.broadcasted_iota(jnp.int32, shape, 1)


def one_hot(condition):
    return condition.astype(F32).astype(BF16)


def over_lanes(a, b):
    return lax.dot_general(a, b, (((1,), (1,)), ((), ())), preferred_element_type=F32)


def split_lanes(values, lanes):
    count = values.shape[1]
    high = values.astype(BF16)
    rest = values - high.astype(F32)
    middle = rest.astype(BF16)
    low = (rest - middle.astype(F32)).astype(BF16)
    k, lane = iotas((count, lanes))
    spread = jnp.dot(high, one_hot(lane == k), preferred_element_type=F32)
    spread = spread + jnp.dot(middle, one_hot(lane == k + count), preferred_element_type=F32)
    spread = spread + jnp.dot(low, one_hot(lane == k + 2 * count), preferred_element_type=F32)
    return spread.astype(BF16)


def join_lanes(parts, count, block, distance):
    k, n = iotas((parts.shape[1], count))
    source = (n // block ^ distance) * block + n % block
    here = (k == source) | (k == source + count) | (k == source + 2 * count)
    return jnp.dot(parts, one_hot(here), preferred_element_type=F32)


def score_kernel(
    particles, sections, own_classes, classes, *refs
):
    messages, (own_ref, sibling_ref, out_ref, listed_ref) = refs[:sections], refs[sections:]
    local_rotations, width, _ = own_ref.shape
    section = lax.axis_index("section")
    held = sections * particles
    spare = messages[0].shape[0] - particles

    coeffs = jnp.concatenate([ref[:particles, :width] for ref in messages], axis=0)
    meta = jnp.concatenate([ref[:particles, width:] for ref in messages], axis=0)
    stack = jnp.concatenate([ref[particles:, :width] for ref in messages], axis=0)

    q, k = iotas((classes, sections * spare))
    row = k % spare
    place = (k // spare ^ section) + row // own_classes * sections
    place = place * own_classes + row % own_classes
    fetched = classes // sections
    refs = jnp.dot(
        one_hot((q == place) & (row < fetched)), stack, preferred_element_type=F32
    ).astype(BF16)

    q, k = iotas((classes + 16, meta.shape[1]))
    turned_meta = over_lanes(one_hot(q == k), meta)
    listed_ref[...] = turned_meta[:classes]
    sharp = turned_meta[classes : classes + 1]
    best = meta[:, classes + 1 : classes + 2].astype(F32)

    turned_refs = jnp.concatenate(
        [
            jnp.dot(refs, rotations_ref[r], preferred_element_type=F32).astype(BF16)
            for rotations_ref in (own_ref, sibling_ref)
            for r in range(local_rotations)
        ],
        axis=0,
    )
    scores = over_lanes(turned_refs, coeffs) * sharp
    scores = scores.reshape(2 * local_rotations, classes, held)
    top = jnp.max(scores, axis=0)
    marg = top + jnp.log(jnp.sum(jnp.exp(scores - top[None]), axis=0))
    out_ref[held:, :] = split_lanes(marg, width)

    wide = coeffs.astype(F32)
    aligned = jnp.zeros((held, width), F32)
    for owner, rotations_ref in ((section, own_ref), (section ^ 1, sibling_ref)):
        offset = best - (owner * local_rotations).astype(F32)
        for r in range(local_rotations):
            chosen = jnp.where(offset == r, wide, 0.0).astype(BF16)
            aligned = aligned + over_lanes(chosen, rotations_ref[r])
    out_ref[:held, :] = aligned.astype(BF16)


def merge(particles, distance, held, mine_ref, theirs_ref):
    slots = held // particles
    theirs = [
        theirs_ref[(m ^ distance) * particles : (m ^ distance) * particles + particles, :]
        for m in range(slots)
    ]
    aligned = mine_ref[:held, :].astype(F32) + jnp.concatenate(theirs, axis=0).astype(F32)
    marg = log_add(
        join_lanes(mine_ref[held:, :], held, particles, 0),
        join_lanes(theirs_ref[held:, :], held, particles, distance),
    )
    return aligned.astype(BF16), marg


def sums_kernel(particles, distance, held, mine_ref, theirs_ref, listed_ref, out_ref, evidence_ref):
    aligned, marg = merge(particles, distance, held, mine_ref, theirs_ref)
    width = aligned.shape[1]
    top = jnp.max(marg, axis=0, keepdims=True)
    raised = jnp.exp(marg - top)
    evidence_ref[...] = top + jnp.log(jnp.sum(raised, axis=0, keepdims=True))
    picked = jnp.where(listed_ref[...] > 0.0, marg, -jnp.inf)
    raised = jnp.exp(picked - jnp.max(picked, axis=0, keepdims=True))
    weights = raised / jnp.sum(raised, axis=0, keepdims=True)
    weights = weights.astype(BF16)
    out_ref[:, :width] = jnp.dot(weights, aligned, preferred_element_type=F32)
    class_weights = jnp.sum(weights.astype(F32), axis=1, keepdims=True)
    out_ref[:, width:] = jnp.broadcast_to(class_weights, (marg.shape[0], LANES))


def small_call(kernel, name, *operands, out_shape, flops=0):
    read = sum(x.size * x.dtype.itemsize for x in operands)
    return pl.pallas_call(
        kernel,
        out_shape=out_shape,
        in_specs=[pl.BlockSpec(memory_space=pltpu.VMEM)] * len(operands),
        out_specs=jax.tree.map(lambda _: pl.BlockSpec(memory_space=pltpu.VMEM), out_shape),
        compiler_params=pltpu.CompilerParams(vmem_limit_bytes=16 * 1024 * 1024),
        cost_estimate=pl.CostEstimate(flops=flops, bytes_accessed=read, transcendentals=0),
        name=name,
    )(*operands)


def body(
    images,
    group_ids,
    row_filters,
    column_filters,
    basis_rows,
    basis_columns,
    rotations,
    references,
    sharpness,
    best_rotation,
    assignments,
):
    particles = images.shape[0]
    sections = lax.axis_size("section")
    owners = lax.axis_size("cls")
    own_classes, width = references.shape
    classes = own_classes * owners
    held = sections * particles

    sibling_rotations = swap(rotations, "section", 1)

    refs = []
    for first in range(0, min(owners, 2 * sections), sections):
        pairs = [
            (s * owners + c, s * owners + (c ^ (first + s or 1)))
            for s in range(sections)
            for c in range(owners)
        ]
        block = lax.ppermute(references, ("section", "cls"), pairs)
        if first == 0:
            block = jnp.where(lax.axis_index("section") == 0, references, block)
        refs.append(block)
    refs = jnp.concatenate(refs, axis=0)
    distance = 2 * sections
    while distance < owners:
        refs = jnp.concatenate([refs, swap(refs, "cls", distance)], axis=0)
        distance *= 2

    message = filter_images(
        images,
        group_ids,
        row_filters,
        column_filters,
        basis_rows,
        basis_columns,
        sharpness,
        best_rotation,
        assignments,
        own_classes,
        classes,
    )
    refs = jnp.pad(refs, ((0, -refs.shape[0] % 16), (0, message.shape[1] - width)))
    message = jnp.concatenate([message, refs], axis=0)
    marg, listed = small_call(
        lambda *r: score_kernel(particles, sections, own_classes, classes, *r),
        "scores",
        message,
        *[swap(message, "section", k) for k in range(1, sections)],
        rotations,
        sibling_rotations,
        out_shape=(
            jax.ShapeDtypeStruct((held + classes, width), BF16),
            jax.ShapeDtypeStruct((classes, held), F32),
        ),
    )

    sums, evidence = small_call(
        lambda *r: sums_kernel(particles, sections - 1, held, *r),
        "class_sums",
        marg,
        swap(marg, "section", sections - 1),
        listed,
        out_shape=(
            jax.ShapeDtypeStruct((classes, width + LANES), F32),
            jax.ShapeDtypeStruct((1, held), F32),
        ),
    )

    distance = owners // 2
    while distance:
        half = distance * own_classes
        sums = sums[:half] + cross(sums[half:], distance)
        distance //= 2
    class_weights = jnp.concatenate([sums[:, width:]] * (width // LANES), axis=1)
    new_references = (sums[:, :width] + references.astype(F32)) / (class_weights + 1.0)
    return new_references, evidence[0, :particles]


def solution(mesh):
    in_specs = (
        P(("section", "cls"), None, None),
        P(("section", "cls")),
        P(),
        P(),
        P(),
        P(),
        P("section", None, None),
        P("cls", None),
        P(("section", "cls")),
        P(("section", "cls")),
        P(("section", "cls"), None),
    )
    out_specs = (P("cls", None), P(("section", "cls")))
    return jax.shard_map(body, mesh=mesh, in_specs=in_specs, out_specs=out_specs, check_vma=False)
```

```python
import math

import jax
import jax.numpy as jnp
import numpy as np
from jax import lax
from jax.experimental import pallas as pl
from jax.experimental.pallas import tpu as pltpu
from jax.sharding import PartitionSpec as P

EPSILON = 1e-05
LANES = 128
FIRST = 4
BF16 = jnp.bfloat16
F32 = jnp.float32


def soft_edge(pixels):
    coordinate = (np.arange(pixels, dtype=np.float32) - (pixels - 1) / 2.0) / (pixels / 2.0)
    radius = np.sqrt(coordinate[:, None] ** 2 + coordinate[None, :] ** 2)
    falloff = np.clip((radius - 0.8) / 0.15, 0.0, 1.0)
    return (0.5 + 0.5 * np.cos(math.pi * falloff)).astype(np.float32)


def filter_kernel(
    own_classes,
    classes,
    groups_ref,
    best_ref,
    images_hbm,
    row_hbm,
    column_hbm,
    mask_hbm,
    basis_rows_ref,
    basis_columns_ref,
    assignments_ref,
    sharp_ref,
    out_ref,
    images_ref,
    row_ref,
    column_ref,
    mask_ref,
    inner,
    sems,
):
    pixels = mask_ref.shape[0]
    row_count = basis_rows_ref.shape[0]
    column_count = basis_columns_ref.shape[0]
    width = row_count * column_count
    particles, message = out_ref.shape

    first = min(FIRST, particles)
    spans = [(0, first), (first, particles - first)]
    fetch_column = pltpu.make_async_copy(column_hbm, column_ref, sems.at[0])
    fetch_row = pltpu.make_async_copy(row_hbm, row_ref, sems.at[1])
    fetch_mask = pltpu.make_async_copy(mask_hbm, mask_ref, sems.at[2])
    fetch_images = [
        pltpu.make_async_copy(
            images_hbm.at[start : start + size], images_ref.at[start : start + size], sems.at[3 + i]
        )
        for i, (start, size) in enumerate(spans)
        if size
    ]
    fetch_column.start()
    fetch_images[0].start()
    fetch_row.start()
    fetch_mask.start()
    for fetch in fetch_images[1:]:
        fetch.start()

    lane = lax.broadcasted_iota(jnp.int32, (column_count, width), 1)
    which = lax.broadcasted_iota(jnp.int32, (column_count, width), 0)
    spread = (lane % column_count == which).astype(F32).astype(BF16)
    wide = lax.dot_general(
        basis_columns_ref[...], spread, (((0,), (0,)), ((), ())), preferred_element_type=F32
    ).astype(BF16)
    lane = lax.broadcasted_iota(jnp.int32, (particles, message - width), 1)
    place = lax.broadcasted_iota(jnp.int32, (particles, message - width), 0)
    named = (lane // own_classes ^ lax.axis_index("cls")) * own_classes + lane % own_classes
    named = jnp.where(lane < classes, named, -1)
    meta = jnp.zeros(lane.shape, F32)
    assignments = assignments_ref[...]
    for j in range(assignments.shape[1]):
        meta = jnp.where(assignments[:, j : j + 1] == named, 1.0, meta)
    square = (particles, particles)
    same = lax.broadcasted_iota(jnp.int32, square, 0) == lax.broadcasted_iota(
        jnp.int32, square, 1
    )
    sharp = jnp.broadcast_to(sharp_ref[...].astype(F32), square)
    sharp = jnp.sum(jnp.where(same, sharp, 0.0), axis=1, keepdims=True)
    meta = jnp.where(lane == classes, sharp, meta)
    for n in range(particles):
        meta = jnp.where(
            (place == n) & (lane == classes + 1), best_ref[n].astype(F32), meta
        )

    for i, fetch in enumerate(fetch_images):
        start, size = spans[i]
        each = range(start, start + size)
        if i == 0:
            fetch_column.wait()
        fetch.wait()
        half = {
            n: jnp.dot(
                images_ref[n], column_ref[groups_ref[n]], preferred_element_type=F32
            ).astype(BF16)
            for n in each
        }
        if i == 0:
            fetch_row.wait()
            fetch_mask.wait()
        scale, masked = {}, {}
        for n in each:
            filtered = jnp.dot(row_ref[groups_ref[n]], half[n], preferred_element_type=F32)
            filtered = filtered * mask_ref[...]
            power = jnp.sum(filtered * filtered, axis=0, keepdims=True)
            power = jnp.sum(power, axis=1, keepdims=True) * (1.0 / (pixels * pixels))
            scale[n] = lax.rsqrt(power + EPSILON)
            masked[n] = filtered.astype(BF16)
        for n in each:
            rows = jnp.dot(basis_rows_ref[...], masked[n], preferred_element_type=F32)
            inner[n * row_count : (n + 1) * row_count, :] = rows * scale[n]

    held = inner[...]
    high = held.astype(BF16)
    low = (held - high.astype(F32)).astype(BF16)
    both = jnp.dot(high, wide, preferred_element_type=F32)
    both = both + jnp.dot(low, wide, preferred_element_type=F32)
    lane = lax.broadcasted_iota(jnp.int32, both.shape, 1)
    which = lax.broadcasted_iota(jnp.int32, both.shape, 0)
    both = jnp.where(lane // column_count == which % row_count, both, 0.0)
    coeffs = jnp.sum(both.reshape(particles, row_count, width), axis=1)

    out_ref[...] = jnp.concatenate([coeffs.astype(BF16), meta.astype(BF16)], axis=1)


def filter_images(
    images,
    group_ids,
    row_filters,
    column_filters,
    basis_rows,
    basis_columns,
    sharpness,
    best_rotation,
    assignments,
    own_classes,
    classes,
):
    particles, pixels = images.shape[:2]
    groups = row_filters.shape[0]
    row_count, column_count = basis_rows.shape[1], basis_columns.shape[1]
    message = row_count * column_count + classes + 2
    message += -message % LANES
    mask = jnp.asarray(soft_edge(pixels))
    anywhere = pl.BlockSpec(memory_space=pl.ANY)
    whole = pl.BlockSpec(memory_space=pltpu.VMEM)
    return pl.pallas_call(
        lambda *refs: filter_kernel(own_classes, classes, *refs),
        out_shape=pltpu.VMEM((particles, message), BF16),
        in_specs=[pl.BlockSpec(memory_space=pltpu.SMEM)] * 2 + [anywhere] * 4 + [whole] * 4,
        out_specs=whole,
        scratch_shapes=[
            pltpu.VMEM(images.shape, BF16),
            pltpu.VMEM(row_filters.shape, BF16),
            pltpu.VMEM(column_filters.shape, BF16),
            pltpu.VMEM((pixels, pixels), F32),
            pltpu.VMEM((particles * row_count, pixels), F32),
            pltpu.SemaphoreType.DMA((5,)),
        ],
        compiler_params=pltpu.CompilerParams(vmem_limit_bytes=60 * 1024 * 1024),
        cost_estimate=pl.CostEstimate(
            flops=4 * particles * pixels**3,
            bytes_accessed=2 * pixels * pixels * (particles + 2 * groups),
            transcendentals=0,
        ),
        name="filter_images",
    )(
        group_ids,
        best_rotation,
        images,
        row_filters,
        column_filters,
        mask,
        basis_rows.T,
        basis_columns.T,
        assignments,
        sharpness.reshape(1, particles),
    )


def cross(array, distance):
    sections, owners = lax.axis_size("section"), lax.axis_size("cls")
    pairs = [
        (s * owners + c, (s ^ 1) * owners + (c ^ distance))
        for s in range(sections)
        for c in range(owners)
    ]
    return lax.ppermute(array, ("section", "cls"), pairs)


def swap(array, axis, distance):
    size = lax.axis_size(axis)
    return lax.ppermute(array, axis, [(i, i ^ distance) for i in range(size)])


def log_add(a, b):
    top = jnp.maximum(a, b)
    return top + jnp.log(jnp.exp(a - top) + jnp.exp(b - top))


def iotas(shape):
    return lax.broadcasted_iota(jnp.int32, shape, 0), lax.broadcasted_iota(jnp.int32, shape, 1)


def one_hot(condition):
    return condition.astype(F32).astype(BF16)


def over_lanes(a, b):
    return lax.dot_general(a, b, (((1,), (1,)), ((), ())), preferred_element_type=F32)


def split_lanes(values, lanes):
    count = values.shape[1]
    high = values.astype(BF16)
    rest = values - high.astype(F32)
    middle = rest.astype(BF16)
    low = (rest - middle.astype(F32)).astype(BF16)
    k, lane = iotas((count, lanes))
    spread = jnp.dot(high, one_hot(lane == k), preferred_element_type=F32)
    spread = spread + jnp.dot(middle, one_hot(lane == k + count), preferred_element_type=F32)
    spread = spread + jnp.dot(low, one_hot(lane == k + 2 * count), preferred_element_type=F32)
    return spread.astype(BF16)


def join_lanes(parts, count, block, distance):
    k, n = iotas((parts.shape[1], count))
    source = (n // block ^ distance) * block + n % block
    here = (k == source) | (k == source + count) | (k == source + 2 * count)
    return jnp.dot(parts, one_hot(here), preferred_element_type=F32)


def score_kernel(
    particles, sections, own_classes, classes, *refs
):
    messages, (own_ref, sibling_ref, out_ref, listed_ref) = refs[:sections], refs[sections:]
    local_rotations, width, _ = own_ref.shape
    section = lax.axis_index("section")
    held = sections * particles
    spare = messages[0].shape[0] - particles

    coeffs = jnp.concatenate([ref[:particles, :width] for ref in messages], axis=0)
    meta = jnp.concatenate([ref[:particles, width:] for ref in messages], axis=0)
    stack = jnp.concatenate([ref[particles:, :width] for ref in messages], axis=0)

    q, k = iotas((classes, sections * spare))
    row = k % spare
    place = (k // spare ^ section ^ sections - 1) + row // own_classes * sections
    place = place * own_classes + row % own_classes
    fetched = classes // sections
    refs = jnp.dot(
        one_hot((q == place) & (row < fetched)), stack, preferred_element_type=F32
    ).astype(BF16)

    q, k = iotas((classes + 16, meta.shape[1]))
    turned_meta = over_lanes(one_hot(q == k), meta)
    listed_ref[...] = turned_meta[:classes]
    sharp = turned_meta[classes : classes + 1]
    best = meta[:, classes + 1 : classes + 2].astype(F32)

    turned_refs = jnp.concatenate(
        [
            jnp.dot(refs, rotations_ref[r], preferred_element_type=F32).astype(BF16)
            for rotations_ref in (own_ref, sibling_ref)
            for r in range(local_rotations)
        ],
        axis=0,
    )
    scores = over_lanes(turned_refs, coeffs) * sharp
    scores = scores.reshape(2 * local_rotations, classes, held)
    top = jnp.max(scores, axis=0)
    marg = top + jnp.log(jnp.sum(jnp.exp(scores - top[None]), axis=0))
    out_ref[held:, :] = split_lanes(marg, width)

    wide = coeffs.astype(F32)
    aligned = jnp.zeros((held, width), F32)
    for owner, rotations_ref in ((section, own_ref), (section ^ 1, sibling_ref)):
        offset = best - (owner * local_rotations).astype(F32)
        for r in range(local_rotations):
            chosen = jnp.where(offset == r, wide, 0.0).astype(BF16)
            aligned = aligned + over_lanes(chosen, rotations_ref[r])
    out_ref[:held, :] = aligned.astype(BF16)


def merge(particles, distance, held, mine_ref, theirs_ref):
    slots = held // particles
    theirs = [
        theirs_ref[(m ^ distance) * particles : (m ^ distance) * particles + particles, :]
        for m in range(slots)
    ]
    aligned = mine_ref[:held, :].astype(F32) + jnp.concatenate(theirs, axis=0).astype(F32)
    marg = log_add(
        join_lanes(mine_ref[held:, :], held, particles, 0),
        join_lanes(theirs_ref[held:, :], held, particles, distance),
    )
    return aligned.astype(BF16), marg


def sums_kernel(particles, distance, held, mine_ref, theirs_ref, listed_ref, out_ref, evidence_ref):
    aligned, marg = merge(particles, distance, held, mine_ref, theirs_ref)
    width = aligned.shape[1]
    top = jnp.max(marg, axis=0, keepdims=True)
    raised = jnp.exp(marg - top)
    evidence_ref[...] = top + jnp.log(jnp.sum(raised, axis=0, keepdims=True))
    picked = jnp.where(listed_ref[...] > 0.0, marg, -jnp.inf)
    raised = jnp.exp(picked - jnp.max(picked, axis=0, keepdims=True))
    weights = raised / jnp.sum(raised, axis=0, keepdims=True)
    weights = weights.astype(BF16)
    out_ref[:, :width] = jnp.dot(weights, aligned, preferred_element_type=F32)
    class_weights = jnp.sum(weights.astype(F32), axis=1, keepdims=True)
    out_ref[:, width:] = jnp.broadcast_to(class_weights, (marg.shape[0], LANES))


def small_call(kernel, name, *operands, out_shape, flops=0):
    read = sum(x.size * x.dtype.itemsize for x in operands)
    return pl.pallas_call(
        kernel,
        out_shape=out_shape,
        in_specs=[pl.BlockSpec(memory_space=pltpu.VMEM)] * len(operands),
        out_specs=jax.tree.map(lambda _: pl.BlockSpec(memory_space=pltpu.VMEM), out_shape),
        compiler_params=pltpu.CompilerParams(vmem_limit_bytes=16 * 1024 * 1024),
        cost_estimate=pl.CostEstimate(flops=flops, bytes_accessed=read, transcendentals=0),
        name=name,
    )(*operands)


def body(
    images,
    group_ids,
    row_filters,
    column_filters,
    basis_rows,
    basis_columns,
    rotations,
    references,
    sharpness,
    best_rotation,
    assignments,
):
    particles = images.shape[0]
    sections = lax.axis_size("section")
    owners = lax.axis_size("cls")
    own_classes, width = references.shape
    classes = own_classes * owners
    held = sections * particles

    sibling_rotations = swap(rotations, "section", 1)

    refs = []
    for first in range(0, min(owners, 2 * sections), sections):
        pairs = [
            (s * owners + c, s * owners + (c ^ (first + sections - 1 - s or 1)))
            for s in range(sections)
            for c in range(owners)
        ]
        block = lax.ppermute(references, ("section", "cls"), pairs)
        if first == 0:
            block = jnp.where(lax.axis_index("section") == sections - 1, references, block)
        refs.append(block)
    refs = jnp.concatenate(refs, axis=0)
    distance = 2 * sections
    while distance < owners:
        refs = jnp.concatenate([refs, swap(refs, "cls", distance)], axis=0)
        distance *= 2

    message = filter_images(
        images,
        group_ids,
        row_filters,
        column_filters,
        basis_rows,
        basis_columns,
        sharpness,
        best_rotation,
        assignments,
        own_classes,
        classes,
    )
    refs = jnp.pad(refs, ((0, -refs.shape[0] % 16), (0, message.shape[1] - width)))
    message = jnp.concatenate([message, refs], axis=0)
    marg, listed = small_call(
        lambda *r: score_kernel(particles, sections, own_classes, classes, *r),
        "scores",
        message,
        *[swap(message, "section", k) for k in range(1, sections)],
        rotations,
        sibling_rotations,
        out_shape=(
            jax.ShapeDtypeStruct((held + classes, width), BF16),
            jax.ShapeDtypeStruct((classes, held), F32),
        ),
    )

    sums, evidence = small_call(
        lambda *r: sums_kernel(particles, sections - 1, held, *r),
        "class_sums",
        marg,
        swap(marg, "section", sections - 1),
        listed,
        out_shape=(
            jax.ShapeDtypeStruct((classes, width + LANES), F32),
            jax.ShapeDtypeStruct((1, held), F32),
        ),
    )

    distance = owners // 2
    while distance:
        half = distance * own_classes
        sums = sums[:half] + cross(sums[half:], distance)
        distance //= 2
    class_weights = jnp.concatenate([sums[:, width:]] * (width // LANES), axis=1)
    new_references = (sums[:, :width] + references.astype(F32)) / (class_weights + 1.0)
    return new_references, evidence[0, :particles]


def solution(mesh):
    in_specs = (
        P(("section", "cls"), None, None),
        P(("section", "cls")),
        P(),
        P(),
        P(),
        P(),
        P("section", None, None),
        P("cls", None),
        P(("section", "cls")),
        P(("section", "cls")),
        P(("section", "cls"), None),
    )
    out_specs = (P("cls", None), P(("section", "cls")))
    return jax.shard_map(body, mesh=mesh, in_specs=in_specs, out_specs=out_specs, check_vma=False)
```

```python
import math

import jax
import jax.numpy as jnp
import numpy as np
from jax import lax
from jax.experimental import pallas as pl
from jax.experimental.pallas import tpu as pltpu
from jax.sharding import PartitionSpec as P

EPSILON = 1e-05
LANES = 128
FIRST = 4
BF16 = jnp.bfloat16
F32 = jnp.float32


def soft_edge(pixels):
    coordinate = (np.arange(pixels, dtype=np.float32) - (pixels - 1) / 2.0) / (pixels / 2.0)
    radius = np.sqrt(coordinate[:, None] ** 2 + coordinate[None, :] ** 2)
    falloff = np.clip((radius - 0.8) / 0.15, 0.0, 1.0)
    return (0.5 + 0.5 * np.cos(math.pi * falloff)).astype(np.float32)


def filter_kernel(
    own_classes,
    classes,
    groups_ref,
    best_ref,
    images_hbm,
    row_hbm,
    column_hbm,
    mask_hbm,
    basis_rows_ref,
    basis_columns_ref,
    assignments_ref,
    sharp_ref,
    out_ref,
    images_ref,
    row_ref,
    column_ref,
    mask_ref,
    inner,
    sems,
):
    pixels = mask_ref.shape[0]
    row_count = basis_rows_ref.shape[0]
    column_count = basis_columns_ref.shape[0]
    width = row_count * column_count
    particles, message = out_ref.shape

    first = min(FIRST, particles)
    spans = [(0, first), (first, particles - first)]
    fetch_column = pltpu.make_async_copy(column_hbm, column_ref, sems.at[0])
    fetch_row = pltpu.make_async_copy(row_hbm, row_ref, sems.at[1])
    fetch_mask = pltpu.make_async_copy(mask_hbm, mask_ref, sems.at[2])
    fetch_images = [
        pltpu.make_async_copy(
            images_hbm.at[start : start + size], images_ref.at[start : start + size], sems.at[3 + i]
        )
        for i, (start, size) in enumerate(spans)
        if size
    ]
    fetch_column.start()
    fetch_images[0].start()
    fetch_row.start()
    fetch_mask.start()
    for fetch in fetch_images[1:]:
        fetch.start()

    lane = lax.broadcasted_iota(jnp.int32, (column_count, width), 1)
    which = lax.broadcasted_iota(jnp.int32, (column_count, width), 0)
    spread = (lane % column_count == which).astype(F32).astype(BF16)
    wide = lax.dot_general(
        basis_columns_ref[...], spread, (((0,), (0,)), ((), ())), preferred_element_type=F32
    ).astype(BF16)
    lane = lax.broadcasted_iota(jnp.int32, (particles, message - width), 1)
    place = lax.broadcasted_iota(jnp.int32, (particles, message - width), 0)
    named = (lane // own_classes ^ lax.axis_index("cls")) * own_classes + lane % own_classes
    named = jnp.where(lane < classes, named, -1)
    meta = jnp.zeros(lane.shape, F32)
    assignments = assignments_ref[...]
    for j in range(assignments.shape[1]):
        meta = jnp.where(assignments[:, j : j + 1] == named, 1.0, meta)
    square = (particles, particles)
    same = lax.broadcasted_iota(jnp.int32, square, 0) == lax.broadcasted_iota(
        jnp.int32, square, 1
    )
    sharp = jnp.broadcast_to(sharp_ref[...].astype(F32), square)
    sharp = jnp.sum(jnp.where(same, sharp, 0.0), axis=1, keepdims=True)
    meta = jnp.where(lane == classes, sharp, meta)
    for n in range(particles):
        meta = jnp.where(
            (place == n) & (lane == classes + 1), best_ref[n].astype(F32), meta
        )

    for i, fetch in enumerate(fetch_images):
        start, size = spans[i]
        each = range(start, start + size)
        if i == 0:
            fetch_column.wait()
        fetch.wait()
        half = {
            n: jnp.dot(
                images_ref[n], column_ref[groups_ref[n]], preferred_element_type=F32
            ).astype(BF16)
            for n in each
        }
        if i == 0:
            fetch_row.wait()
            fetch_mask.wait()
        scale, masked = {}, {}
        for n in each:
            filtered = jnp.dot(row_ref[groups_ref[n]], half[n], preferred_element_type=F32)
            filtered = filtered * mask_ref[...]
            power = jnp.sum(filtered * filtered, axis=0, keepdims=True)
            power = jnp.sum(power, axis=1, keepdims=True) * (1.0 / (pixels * pixels))
            scale[n] = lax.rsqrt(power + EPSILON)
            masked[n] = filtered.astype(BF16)
        for n in each:
            rows = jnp.dot(basis_rows_ref[...], masked[n], preferred_element_type=F32)
            inner[n * row_count : (n + 1) * row_count, :] = rows * scale[n]

    held = inner[...]
    high = held.astype(BF16)
    low = (held - high.astype(F32)).astype(BF16)
    both = jnp.dot(high, wide, preferred_element_type=F32)
    both = both + jnp.dot(low, wide, preferred_element_type=F32)
    lane = lax.broadcasted_iota(jnp.int32, both.shape, 1)
    which = lax.broadcasted_iota(jnp.int32, both.shape, 0)
    both = jnp.where(lane // column_count == which % row_count, both, 0.0)
    coeffs = jnp.sum(both.reshape(particles, row_count, width), axis=1)

    out_ref[...] = jnp.concatenate([coeffs.astype(BF16), meta.astype(BF16)], axis=1)


def filter_images(
    images,
    group_ids,
    row_filters,
    column_filters,
    basis_rows,
    basis_columns,
    sharpness,
    best_rotation,
    assignments,
    own_classes,
    classes,
):
    particles, pixels = images.shape[:2]
    groups = row_filters.shape[0]
    row_count, column_count = basis_rows.shape[1], basis_columns.shape[1]
    message = row_count * column_count + classes + 2
    message += -message % LANES
    mask = jnp.asarray(soft_edge(pixels))
    anywhere = pl.BlockSpec(memory_space=pl.ANY)
    whole = pl.BlockSpec(memory_space=pltpu.VMEM)
    return pl.pallas_call(
        lambda *refs: filter_kernel(own_classes, classes, *refs),
        out_shape=pltpu.VMEM((particles, message), BF16),
        in_specs=[pl.BlockSpec(memory_space=pltpu.SMEM)] * 2 + [anywhere] * 4 + [whole] * 4,
        out_specs=whole,
        scratch_shapes=[
            pltpu.VMEM(images.shape, BF16),
            pltpu.VMEM(row_filters.shape, BF16),
            pltpu.VMEM(column_filters.shape, BF16),
            pltpu.VMEM((pixels, pixels), F32),
            pltpu.VMEM((particles * row_count, pixels), F32),
            pltpu.SemaphoreType.DMA((5,)),
        ],
        compiler_params=pltpu.CompilerParams(vmem_limit_bytes=60 * 1024 * 1024),
        cost_estimate=pl.CostEstimate(
            flops=4 * particles * pixels**3,
            bytes_accessed=2 * pixels * pixels * (particles + 2 * groups),
            transcendentals=0,
        ),
        name="filter_images",
    )(
        group_ids,
        best_rotation,
        images,
        row_filters,
        column_filters,
        mask,
        basis_rows.T,
        basis_columns.T,
        assignments,
        sharpness.reshape(1, particles),
    )


def cross(array, distance):
    sections, owners = lax.axis_size("section"), lax.axis_size("cls")
    pairs = [
        (s * owners + c, (s ^ 1) * owners + (c ^ distance))
        for s in range(sections)
        for c in range(owners)
    ]
    return lax.ppermute(array, ("section", "cls"), pairs)


def swap(array, axis, distance):
    size = lax.axis_size(axis)
    return lax.ppermute(array, axis, [(i, i ^ distance) for i in range(size)])


def log_add(a, b):
    top = jnp.maximum(a, b)
    return top + jnp.log(jnp.exp(a - top) + jnp.exp(b - top))


def iotas(shape):
    return lax.broadcasted_iota(jnp.int32, shape, 0), lax.broadcasted_iota(jnp.int32, shape, 1)


def one_hot(condition):
    return condition.astype(F32).astype(BF16)


def over_lanes(a, b):
    return lax.dot_general(a, b, (((1,), (1,)), ((), ())), preferred_element_type=F32)


def split_lanes(values, lanes):
    count = values.shape[1]
    high = values.astype(BF16)
    rest = values - high.astype(F32)
    middle = rest.astype(BF16)
    low = (rest - middle.astype(F32)).astype(BF16)
    k, lane = iotas((count, lanes))
    spread = jnp.dot(high, one_hot(lane == k), preferred_element_type=F32)
    spread = spread + jnp.dot(middle, one_hot(lane == k + count), preferred_element_type=F32)
    spread = spread + jnp.dot(low, one_hot(lane == k + 2 * count), preferred_element_type=F32)
    return spread.astype(BF16)


def join_lanes(parts, count, block, distance):
    k, n = iotas((parts.shape[1], count))
    source = (n // block ^ distance) * block + n % block
    here = (k == source) | (k == source + count) | (k == source + 2 * count)
    return jnp.dot(parts, one_hot(here), preferred_element_type=F32)


def score_kernel(
    particles, order, own_classes, classes, *refs
):
    sections = len(order)
    own_ref, sibling_ref, out_ref, listed_ref = refs[sections:]
    messages = [refs[order.index(m)] for m in range(sections)]
    local_rotations, width, _ = own_ref.shape
    section = lax.axis_index("section")
    held = sections * particles
    spare = messages[0].shape[0] - particles

    coeffs = jnp.concatenate([ref[:particles, :width] for ref in messages], axis=0)
    meta = jnp.concatenate([ref[:particles, width:] for ref in messages], axis=0)
    stack = jnp.concatenate([ref[particles:, :width] for ref in messages], axis=0)

    q, k = iotas((classes, sections * spare))
    row = k % spare
    place = (k // spare ^ section ^ sections - 1) + row // own_classes * sections
    place = place * own_classes + row % own_classes
    fetched = classes // sections
    refs = jnp.dot(
        one_hot((q == place) & (row < fetched)), stack, preferred_element_type=F32
    ).astype(BF16)

    q, k = iotas((classes + 16, meta.shape[1]))
    turned_meta = over_lanes(one_hot(q == k), meta)
    listed_ref[...] = turned_meta[:classes]
    sharp = turned_meta[classes : classes + 1]
    best = meta[:, classes + 1 : classes + 2].astype(F32)

    turned_refs = jnp.concatenate(
        [
            jnp.dot(refs, rotations_ref[r], preferred_element_type=F32).astype(BF16)
            for rotations_ref in (own_ref, sibling_ref)
            for r in range(local_rotations)
        ],
        axis=0,
    )
    scores = over_lanes(turned_refs, coeffs) * sharp
    scores = scores.reshape(2 * local_rotations, classes, held)
    top = jnp.max(scores, axis=0)
    marg = top + jnp.log(jnp.sum(jnp.exp(scores - top[None]), axis=0))
    out_ref[held:, :] = split_lanes(marg, width)

    wide = coeffs.astype(F32)
    aligned = jnp.zeros((held, width), F32)
    for owner, rotations_ref in ((section, own_ref), (section ^ 1, sibling_ref)):
        offset = best - (owner * local_rotations).astype(F32)
        for r in range(local_rotations):
            chosen = jnp.where(offset == r, wide, 0.0).astype(BF16)
            aligned = aligned + over_lanes(chosen, rotations_ref[r])
    out_ref[:held, :] = aligned.astype(BF16)


def merge(particles, distance, held, mine_ref, theirs_ref):
    slots = held // particles
    theirs = [
        theirs_ref[(m ^ distance) * particles : (m ^ distance) * particles + particles, :]
        for m in range(slots)
    ]
    aligned = mine_ref[:held, :].astype(F32) + jnp.concatenate(theirs, axis=0).astype(F32)
    marg = log_add(
        join_lanes(mine_ref[held:, :], held, particles, 0),
        join_lanes(theirs_ref[held:, :], held, particles, distance),
    )
    return aligned.astype(BF16), marg


def sums_kernel(particles, distance, held, mine_ref, theirs_ref, listed_ref, out_ref, evidence_ref):
    aligned, marg = merge(particles, distance, held, mine_ref, theirs_ref)
    width = aligned.shape[1]
    top = jnp.max(marg, axis=0, keepdims=True)
    raised = jnp.exp(marg - top)
    evidence_ref[...] = top + jnp.log(jnp.sum(raised, axis=0, keepdims=True))
    picked = jnp.where(listed_ref[...] > 0.0, marg, -jnp.inf)
    raised = jnp.exp(picked - jnp.max(picked, axis=0, keepdims=True))
    weights = raised / jnp.sum(raised, axis=0, keepdims=True)
    weights = weights.astype(BF16)
    out_ref[:, :width] = jnp.dot(weights, aligned, preferred_element_type=F32)
    class_weights = jnp.sum(weights.astype(F32), axis=1, keepdims=True)
    out_ref[:, width:] = jnp.broadcast_to(class_weights, (marg.shape[0], LANES))


def small_call(kernel, name, *operands, out_shape, flops=0):
    read = sum(x.size * x.dtype.itemsize for x in operands)
    return pl.pallas_call(
        kernel,
        out_shape=out_shape,
        in_specs=[pl.BlockSpec(memory_space=pltpu.VMEM)] * len(operands),
        out_specs=jax.tree.map(lambda _: pl.BlockSpec(memory_space=pltpu.VMEM), out_shape),
        compiler_params=pltpu.CompilerParams(vmem_limit_bytes=16 * 1024 * 1024),
        cost_estimate=pl.CostEstimate(flops=flops, bytes_accessed=read, transcendentals=0),
        name=name,
    )(*operands)


def body(
    images,
    group_ids,
    row_filters,
    column_filters,
    basis_rows,
    basis_columns,
    rotations,
    references,
    sharpness,
    best_rotation,
    assignments,
):
    particles = images.shape[0]
    sections = lax.axis_size("section")
    owners = lax.axis_size("cls")
    own_classes, width = references.shape
    classes = own_classes * owners
    held = sections * particles

    sibling_rotations = swap(rotations, "section", 1)

    refs = []
    for first in range(0, min(owners, 2 * sections), sections):
        pairs = [
            (s * owners + c, s * owners + (c ^ (first + sections - 1 - s or 1)))
            for s in range(sections)
            for c in range(owners)
        ]
        block = lax.ppermute(references, ("section", "cls"), pairs)
        if first == 0:
            block = jnp.where(lax.axis_index("section") == sections - 1, references, block)
        refs.append(block)
    refs = jnp.concatenate(refs, axis=0)
    distance = 2 * sections
    while distance < owners:
        refs = jnp.concatenate([refs, swap(refs, "cls", distance)], axis=0)
        distance *= 2

    message = filter_images(
        images,
        group_ids,
        row_filters,
        column_filters,
        basis_rows,
        basis_columns,
        sharpness,
        best_rotation,
        assignments,
        own_classes,
        classes,
    )
    refs = jnp.pad(refs, ((0, -refs.shape[0] % 16), (0, message.shape[1] - width)))
    message = jnp.concatenate([message, refs], axis=0)
    order = [*range(1, sections, 2), *range(2, sections, 2)]
    marg, listed = small_call(
        lambda *r: score_kernel(particles, [0, *order], own_classes, classes, *r),
        "scores",
        message,
        *[swap(message, "section", k) for k in order],
        rotations,
        sibling_rotations,
        out_shape=(
            jax.ShapeDtypeStruct((held + classes, width), BF16),
            jax.ShapeDtypeStruct((classes, held), F32),
        ),
    )

    sums, evidence = small_call(
        lambda *r: sums_kernel(particles, sections - 1, held, *r),
        "class_sums",
        marg,
        swap(marg, "section", sections - 1),
        listed,
        out_shape=(
            jax.ShapeDtypeStruct((classes, width + LANES), F32),
            jax.ShapeDtypeStruct((1, held), F32),
        ),
    )

    distance = owners // 2
    while distance:
        half = distance * own_classes
        sums = sums[:half] + cross(sums[half:], distance)
        distance //= 2
    class_weights = jnp.concatenate([sums[:, width:]] * (width // LANES), axis=1)
    new_references = (sums[:, :width] + references.astype(F32)) / (class_weights + 1.0)
    return new_references, evidence[0, :particles]


def solution(mesh):
    in_specs = (
        P(("section", "cls"), None, None),
        P(("section", "cls")),
        P(),
        P(),
        P(),
        P(),
        P("section", None, None),
        P("cls", None),
        P(("section", "cls")),
        P(("section", "cls")),
        P(("section", "cls"), None),
    )
    out_specs = (P("cls", None), P(("section", "cls")))
    return jax.shard_map(body, mesh=mesh, in_specs=in_specs, out_specs=out_specs, check_vma=False)
```

```python
import math

import jax
import jax.numpy as jnp
import numpy as np
from jax import lax
from jax.experimental import pallas as pl
from jax.experimental.pallas import tpu as pltpu
from jax.sharding import PartitionSpec as P

EPSILON = 1e-05
LANES = 128
FIRST = 4
BF16 = jnp.bfloat16
F32 = jnp.float32


def soft_edge(pixels):
    coordinate = (np.arange(pixels, dtype=np.float32) - (pixels - 1) / 2.0) / (pixels / 2.0)
    radius = np.sqrt(coordinate[:, None] ** 2 + coordinate[None, :] ** 2)
    falloff = np.clip((radius - 0.8) / 0.15, 0.0, 1.0)
    return (0.5 + 0.5 * np.cos(math.pi * falloff)).astype(np.float32)


def filter_kernel(
    own_classes,
    classes,
    groups_ref,
    best_ref,
    images_hbm,
    row_hbm,
    column_hbm,
    mask_hbm,
    basis_rows_ref,
    basis_columns_ref,
    assignments_ref,
    sharp_ref,
    out_ref,
    images_ref,
    row_ref,
    column_ref,
    mask_ref,
    inner,
    sems,
):
    pixels = mask_ref.shape[0]
    row_count = basis_rows_ref.shape[0]
    column_count = basis_columns_ref.shape[0]
    width = row_count * column_count
    particles, message = out_ref.shape

    first = min(FIRST, particles)
    spans = [(0, first), (first, particles - first)]
    fetch_column = pltpu.make_async_copy(column_hbm, column_ref, sems.at[0])
    fetch_row = pltpu.make_async_copy(row_hbm, row_ref, sems.at[1])
    fetch_mask = pltpu.make_async_copy(mask_hbm, mask_ref, sems.at[2])
    fetch_images = [
        pltpu.make_async_copy(
            images_hbm.at[start : start + size], images_ref.at[start : start + size], sems.at[3 + i]
        )
        for i, (start, size) in enumerate(spans)
        if size
    ]
    fetch_column.start()
    fetch_images[0].start()
    fetch_row.start()
    fetch_mask.start()
    for fetch in fetch_images[1:]:
        fetch.start()

    lane = lax.broadcasted_iota(jnp.int32, (column_count, width), 1)
    which = lax.broadcasted_iota(jnp.int32, (column_count, width), 0)
    spread = (lane % column_count == which).astype(F32).astype(BF16)
    wide = lax.dot_general(
        basis_columns_ref[...], spread, (((0,), (0,)), ((), ())), preferred_element_type=F32
    ).astype(BF16)
    lane = lax.broadcasted_iota(jnp.int32, (particles, message - width), 1)
    place = lax.broadcasted_iota(jnp.int32, (particles, message - width), 0)
    named = (lane // own_classes ^ lax.axis_index("cls")) * own_classes + lane % own_classes
    named = jnp.where(lane < classes, named, -1)
    meta = jnp.zeros(lane.shape, F32)
    assignments = assignments_ref[...]
    for j in range(assignments.shape[1]):
        meta = jnp.where(assignments[:, j : j + 1] == named, 1.0, meta)
    square = (particles, particles)
    same = lax.broadcasted_iota(jnp.int32, square, 0) == lax.broadcasted_iota(
        jnp.int32, square, 1
    )
    sharp = jnp.broadcast_to(sharp_ref[...].astype(F32), square)
    sharp = jnp.sum(jnp.where(same, sharp, 0.0), axis=1, keepdims=True)
    meta = jnp.where(lane == classes, sharp, meta)
    for n in range(particles):
        meta = jnp.where(
            (place == n) & (lane == classes + 1), best_ref[n].astype(F32), meta
        )

    for i, fetch in enumerate(fetch_images):
        start, size = spans[i]
        each = range(start, start + size)
        if i == 0:
            fetch_column.wait()
        fetch.wait()
        half = {
            n: jnp.dot(
                images_ref[n], column_ref[groups_ref[n]], preferred_element_type=F32
            ).astype(BF16)
            for n in each
        }
        if i == 0:
            fetch_row.wait()
            fetch_mask.wait()
        scale, masked = {}, {}
        for n in each:
            filtered = jnp.dot(row_ref[groups_ref[n]], half[n], preferred_element_type=F32)
            filtered = filtered * mask_ref[...]
            power = jnp.sum(filtered * filtered, axis=0, keepdims=True)
            power = jnp.sum(power, axis=1, keepdims=True) * (1.0 / (pixels * pixels))
            scale[n] = lax.rsqrt(power + EPSILON)
            masked[n] = filtered.astype(BF16)
        for n in each:
            rows = jnp.dot(basis_rows_ref[...], masked[n], preferred_element_type=F32)
            inner[n * row_count : (n + 1) * row_count, :] = rows * scale[n]

    held = inner[...]
    high = held.astype(BF16)
    low = (held - high.astype(F32)).astype(BF16)
    both = jnp.dot(high, wide, preferred_element_type=F32)
    both = both + jnp.dot(low, wide, preferred_element_type=F32)
    lane = lax.broadcasted_iota(jnp.int32, both.shape, 1)
    which = lax.broadcasted_iota(jnp.int32, both.shape, 0)
    both = jnp.where(lane // column_count == which % row_count, both, 0.0)
    coeffs = jnp.sum(both.reshape(particles, row_count, width), axis=1)

    out_ref[...] = jnp.concatenate([coeffs.astype(BF16), meta.astype(BF16)], axis=1)


def filter_images(
    images,
    group_ids,
    row_filters,
    column_filters,
    basis_rows,
    basis_columns,
    sharpness,
    best_rotation,
    assignments,
    own_classes,
    classes,
):
    particles, pixels = images.shape[:2]
    groups = row_filters.shape[0]
    row_count, column_count = basis_rows.shape[1], basis_columns.shape[1]
    message = row_count * column_count + classes + 2
    message += -message % LANES
    mask = jnp.asarray(soft_edge(pixels))
    anywhere = pl.BlockSpec(memory_space=pl.ANY)
    whole = pl.BlockSpec(memory_space=pltpu.VMEM)
    return pl.pallas_call(
        lambda *refs: filter_kernel(own_classes, classes, *refs),
        out_shape=pltpu.VMEM((particles, message), BF16),
        in_specs=[pl.BlockSpec(memory_space=pltpu.SMEM)] * 2 + [anywhere] * 4 + [whole] * 4,
        out_specs=whole,
        scratch_shapes=[
            pltpu.VMEM(images.shape, BF16),
            pltpu.VMEM(row_filters.shape, BF16),
            pltpu.VMEM(column_filters.shape, BF16),
            pltpu.VMEM((pixels, pixels), F32),
            pltpu.VMEM((particles * row_count, pixels), F32),
            pltpu.SemaphoreType.DMA((5,)),
        ],
        compiler_params=pltpu.CompilerParams(vmem_limit_bytes=60 * 1024 * 1024),
        cost_estimate=pl.CostEstimate(
            flops=4 * particles * pixels**3,
            bytes_accessed=2 * pixels * pixels * (particles + 2 * groups),
            transcendentals=0,
        ),
        name="filter_images",
    )(
        group_ids,
        best_rotation,
        images,
        row_filters,
        column_filters,
        mask,
        basis_rows.T,
        basis_columns.T,
        assignments,
        sharpness.reshape(1, particles),
    )


def cross(array, distance):
    sections, owners = lax.axis_size("section"), lax.axis_size("cls")
    pairs = [
        (s * owners + c, (s ^ 1) * owners + (c ^ distance))
        for s in range(sections)
        for c in range(owners)
    ]
    return lax.ppermute(array, ("section", "cls"), pairs)


def swap(array, axis, distance):
    size = lax.axis_size(axis)
    return lax.ppermute(array, axis, [(i, i ^ distance) for i in range(size)])


def log_add(a, b):
    top = jnp.maximum(a, b)
    return top + jnp.log(jnp.exp(a - top) + jnp.exp(b - top))


def iotas(shape):
    return lax.broadcasted_iota(jnp.int32, shape, 0), lax.broadcasted_iota(jnp.int32, shape, 1)


def one_hot(condition):
    return condition.astype(F32).astype(BF16)


def over_lanes(a, b):
    return lax.dot_general(a, b, (((1,), (1,)), ((), ())), preferred_element_type=F32)


def split_lanes(values, lanes):
    count = values.shape[1]
    high = values.astype(BF16)
    rest = values - high.astype(F32)
    middle = rest.astype(BF16)
    low = (rest - middle.astype(F32)).astype(BF16)
    k, lane = iotas((count, lanes))
    spread = jnp.dot(high, one_hot(lane == k), preferred_element_type=F32)
    spread = spread + jnp.dot(middle, one_hot(lane == k + count), preferred_element_type=F32)
    spread = spread + jnp.dot(low, one_hot(lane == k + 2 * count), preferred_element_type=F32)
    return spread.astype(BF16)


def join_lanes(parts, count, block, distance):
    k, n = iotas((parts.shape[1], count))
    source = (n // block ^ distance) * block + n % block
    here = (k == source) | (k == source + count) | (k == source + 2 * count)
    return jnp.dot(parts, one_hot(here), preferred_element_type=F32)


def score_kernel(
    particles, sections, own_classes, classes, *refs
):
    messages, (own_ref, sibling_ref, out_ref, listed_ref) = refs[:sections], refs[sections:]
    local_rotations, width, _ = own_ref.shape
    section = lax.axis_index("section")
    held = sections * particles
    spare = messages[0].shape[0] - particles

    coeffs = jnp.concatenate([ref[:particles, :width] for ref in messages], axis=0)
    meta = jnp.concatenate([ref[:particles, width:] for ref in messages], axis=0)
    stack = jnp.concatenate([ref[particles:, :width] for ref in messages], axis=0)

    q, k = iotas((classes, sections * spare))
    row = k % spare
    place = (k // spare ^ section ^ sections - 1) + row // own_classes * sections
    place = place * own_classes + row % own_classes
    fetched = classes // sections
    refs = jnp.dot(
        one_hot((q == place) & (row < fetched)), stack, preferred_element_type=F32
    ).astype(BF16)

    q, k = iotas((classes + 16, meta.shape[1]))
    turned_meta = over_lanes(one_hot(q == k), meta)
    listed_ref[...] = turned_meta[:classes]
    sharp = turned_meta[classes : classes + 1]
    best = meta[:, classes + 1 : classes + 2].astype(F32)

    turned_refs = jnp.concatenate(
        [
            jnp.dot(refs, rotations_ref[r], preferred_element_type=F32).astype(BF16)
            for rotations_ref in (own_ref, sibling_ref)
            for r in range(local_rotations)
        ],
        axis=0,
    )
    scores = over_lanes(turned_refs, coeffs) * sharp
    scores = scores.reshape(2 * local_rotations, classes, held)
    top = jnp.max(scores, axis=0)
    marg = top + jnp.log(jnp.sum(jnp.exp(scores - top[None]), axis=0))
    out_ref[held:, :] = split_lanes(marg, width)

    wide = coeffs.astype(F32)
    aligned = jnp.zeros((held, width), F32)
    for owner, rotations_ref in ((section, own_ref), (section ^ 1, sibling_ref)):
        offset = best - (owner * local_rotations).astype(F32)
        for r in range(local_rotations):
            chosen = jnp.where(offset == r, wide, 0.0).astype(BF16)
            aligned = aligned + over_lanes(chosen, rotations_ref[r])
    out_ref[:held, :] = aligned.astype(BF16)


def merge(particles, distance, held, mine_ref, theirs_ref):
    slots = held // particles
    theirs = [
        theirs_ref[(m ^ distance) * particles : (m ^ distance) * particles + particles, :]
        for m in range(slots)
    ]
    aligned = mine_ref[:held, :].astype(F32) + jnp.concatenate(theirs, axis=0).astype(F32)
    marg = log_add(
        join_lanes(mine_ref[held:, :], held, particles, 0),
        join_lanes(theirs_ref[held:, :], held, particles, distance),
    )
    return aligned.astype(BF16), marg


def sums_kernel(particles, distance, held, mine_ref, theirs_ref, listed_ref, out_ref, evidence_ref):
    aligned, marg = merge(particles, distance, held, mine_ref, theirs_ref)
    width = aligned.shape[1]
    top = jnp.max(marg, axis=0, keepdims=True)
    raised = jnp.exp(marg - top)
    evidence_ref[...] = top + jnp.log(jnp.sum(raised, axis=0, keepdims=True))
    picked = jnp.where(listed_ref[...] > 0.0, marg, -jnp.inf)
    raised = jnp.exp(picked - jnp.max(picked, axis=0, keepdims=True))
    weights = raised / jnp.sum(raised, axis=0, keepdims=True)
    weights = weights.astype(BF16)
    out_ref[:, :width] = jnp.dot(weights, aligned, preferred_element_type=F32)
    class_weights = jnp.sum(weights.astype(F32), axis=1, keepdims=True)
    out_ref[:, width:] = jnp.broadcast_to(class_weights, (marg.shape[0], LANES))


def small_call(kernel, name, *operands, out_shape, flops=0):
    read = sum(x.size * x.dtype.itemsize for x in operands)
    return pl.pallas_call(
        kernel,
        out_shape=out_shape,
        in_specs=[pl.BlockSpec(memory_space=pltpu.VMEM)] * len(operands),
        out_specs=jax.tree.map(lambda _: pl.BlockSpec(memory_space=pltpu.VMEM), out_shape),
        compiler_params=pltpu.CompilerParams(vmem_limit_bytes=16 * 1024 * 1024),
        cost_estimate=pl.CostEstimate(flops=flops, bytes_accessed=read, transcendentals=0),
        name=name,
    )(*operands)


def body(
    images,
    group_ids,
    row_filters,
    column_filters,
    basis_rows,
    basis_columns,
    rotations,
    references,
    sharpness,
    best_rotation,
    assignments,
):
    particles = images.shape[0]
    sections = lax.axis_size("section")
    owners = lax.axis_size("cls")
    own_classes, width = references.shape
    classes = own_classes * owners
    held = sections * particles

    sibling_rotations = swap(rotations, "section", 1)

    refs = []
    for first in range(0, min(owners, 2 * sections), sections):
        pairs = [
            (s * owners + c, s * owners + (c ^ (first + sections - 1 - s or 1)))
            for s in range(sections)
            for c in range(owners)
        ]
        block = lax.ppermute(references, ("section", "cls"), pairs)
        if first == 0:
            block = jnp.where(lax.axis_index("section") == sections - 1, references, block)
        refs.append(block)
    refs = jnp.concatenate(refs, axis=0)
    distance = 2 * sections
    while distance < owners:
        refs = jnp.concatenate([refs, swap(refs, "cls", distance)], axis=0)
        distance *= 2

    message = filter_images(
        images,
        group_ids,
        row_filters,
        column_filters,
        basis_rows,
        basis_columns,
        sharpness,
        best_rotation,
        assignments,
        own_classes,
        classes,
    )
    refs = jnp.pad(refs, ((0, -refs.shape[0] % 16), (0, message.shape[1] - width)))
    message = jnp.concatenate([message, refs], axis=0)
    others = {k: swap(message, "section", k) for k in range(1, sections, 2)}
    for k in range(2, sections, 2):
        others[k] = swap(others[k ^ 1], "section", 1)
    marg, listed = small_call(
        lambda *r: score_kernel(particles, sections, own_classes, classes, *r),
        "scores",
        message,
        *[others[k] for k in range(1, sections)],
        rotations,
        sibling_rotations,
        out_shape=(
            jax.ShapeDtypeStruct((held + classes, width), BF16),
            jax.ShapeDtypeStruct((classes, held), F32),
        ),
    )

    sums, evidence = small_call(
        lambda *r: sums_kernel(particles, sections - 1, held, *r),
        "class_sums",
        marg,
        swap(marg, "section", sections - 1),
        listed,
        out_shape=(
            jax.ShapeDtypeStruct((classes, width + LANES), F32),
            jax.ShapeDtypeStruct((1, held), F32),
        ),
    )

    distance = owners // 2
    while distance:
        half = distance * own_classes
        sums = sums[:half] + cross(sums[half:], distance)
        distance //= 2
    class_weights = jnp.concatenate([sums[:, width:]] * (width // LANES), axis=1)
    new_references = (sums[:, :width] + references.astype(F32)) / (class_weights + 1.0)
    return new_references, evidence[0, :particles]


def solution(mesh):
    in_specs = (
        P(("section", "cls"), None, None),
        P(("section", "cls")),
        P(),
        P(),
        P(),
        P(),
        P("section", None, None),
        P("cls", None),
        P(("section", "cls")),
        P(("section", "cls")),
        P(("section", "cls"), None),
    )
    out_specs = (P("cls", None), P(("section", "cls")))
    return jax.shard_map(body, mesh=mesh, in_specs=in_specs, out_specs=out_specs, check_vma=False)
```
